32 devices in a mesh: row: 4 (over z), col: 8 (over y, x, core).
Axes of the slice: x: 2, y: 2, z: 4, core: 2. Of those that a mesh axis runs over, the one named last changes fastest.
Arguments:
- coeffs: float32 [4096, 4096], P('row', 'col'), may hold values from -6 to 6
- hamiltonian_tiles: float32 [8, 4, 512, 512], P('col'), may hold values from -0.125 to 0.125
- source_lists: int32 [8, 3], P('col'), may hold values from 0 to 7, as said below
- present: int32 [8, 4, 4, 4], P('col'), may hold values 0 or 1
Outputs:
- sigma_vector: float32 [4096, 4096], P('row', 'col')
The draws below stay inside these ranges and needn't reach their ends.
Inputs may be any that keep to these rules, and one draw needn't show every extreme that they name: `source_lists`: each row names 3 different tiles, never its own; every tile is named by some row.
All inputs are finite; a program needn't handle non-finite values. No bound on the sum of `present` on one device may be relied on, other than what follows from the above.
Results may differ from the reference program's by a relative error of at most 0.0003.
Values sent between devices are 32-bit elements; how exact they have to be, the bound alone decides.
A program may use at most 192 MiB of HBM per device.

```python
import jax
import jax.numpy as jnp
from jax import lax

TILE_STRINGS = 512
BLOCK_STRINGS = 128
SLOT_COUNT = 4
TILE_COUNT = 8
W = 4096


def draw_source_lists(key, part):
    first_key = jax.random.fold_in(key, 11)
    second_key = jax.random.fold_in(key, 23)
    cycle_order = jax.random.permutation(first_key, TILE_COUNT).astype(jnp.int32)
    following = jnp.roll(cycle_order, -1)
    first_listed = jnp.zeros((TILE_COUNT,), jnp.int32).at[cycle_order].set(following)
    positions = jnp.arange(TILE_COUNT, dtype=jnp.int32)
    scores = jax.random.randint(second_key, (TILE_COUNT, TILE_COUNT), 0, 1 << 20, dtype=jnp.int32) * TILE_COUNT + positions[None, :]
    banned = (positions[None, :] == positions[:, None]) | (positions[None, :] == first_listed[:, None])
    scores = jnp.where(banned, -1, scores)
    ranking = jnp.argsort(-scores, axis=1, stable=True).astype(jnp.int32)
    return jnp.stack([first_listed, ranking[:, 0], ranking[:, 1]], axis=1).astype(jnp.int32)


def with_ends(drawn, stream_key, low, largest):
    longest = drawn.shape.index(max(drawn.shape))
    spots = []
    for shift in (0, 1):
        where = [jax.random.randint(jax.random.fold_in(stream_key, axis), (), 0, length) for axis, length in enumerate(drawn.shape)]
        where[longest] = (where[longest] + shift) % drawn.shape[longest]
        spots.append(tuple(where))
    return drawn.at[spots[0]].set(low).at[spots[1]].set(largest)


def shard_levels(rng, dims, split, low, largest):
    factor_of = 1.0
    for axis_at, blocks in split:
        draws = jax.random.uniform(jax.random.fold_in(jax.random.fold_in(rng, 6), axis_at), (blocks,), jnp.float32, low / len(split), largest / len(split))
        factor_of = factor_of * jnp.repeat(jnp.exp(draws), dims[axis_at] // blocks).reshape((-1,) + (1,) * (len(dims) - 1 - axis_at))
    return factor_of


def centred(rng, dims, deviation, most, cuts=(), held_as=jnp.bfloat16):
    level = shard_levels(rng, dims, cuts, -0.22, 0.18) if cuts else 1.0
    entries = jax.random.normal(rng, dims, jnp.float32) * deviation * level
    return jnp.minimum(jnp.maximum(entries, -most), most).astype(held_as)


def setup_inputs(seed: int = 0) -> dict:
    keys = jax.random.split(jax.random.key(seed), 5)
    coeffs = centred(keys[0], (W, W), 1.0, 6.0, ((0, 4), (1, 8)), jnp.float32)
    hamiltonian_tiles = centred(keys[1], (TILE_COUNT, SLOT_COUNT, TILE_STRINGS, TILE_STRINGS), (SLOT_COUNT * TILE_STRINGS) ** -0.5, 0.125, ((0, 8),), jnp.float32)
    source_lists = draw_source_lists(jax.random.fold_in(keys[4], 71), 0)
    present = with_ends((jax.random.randint(keys[3], (TILE_COUNT, SLOT_COUNT, TILE_STRINGS // BLOCK_STRINGS, TILE_STRINGS // BLOCK_STRINGS), 0, 5) < 4).astype(jnp.int32), jax.random.fold_in(keys[3], 1), 0, 1)
    return dict(coeffs=coeffs, hamiltonian_tiles=hamiltonian_tiles, source_lists=source_lists, present=present)


def expand_mask(present_tile):
    return jnp.repeat(jnp.repeat(present_tile, BLOCK_STRINGS, axis=-2), BLOCK_STRINGS, axis=-1)


def product(left, right):
    return jnp.dot(left, right, precision=lax.Precision.HIGHEST, preferred_element_type=jnp.float32)


def reference(coeffs, hamiltonian_tiles, source_lists, present):
    masked = hamiltonian_tiles * expand_mask(present).astype(jnp.float32)

    def one_column(column):
        sources = jnp.concatenate([column[None].astype(jnp.int32), source_lists[column].astype(jnp.int32)])
        blocks = masked[column]
        total = jnp.zeros((W, TILE_STRINGS), jnp.float32)
        for index_of_slot in range(SLOT_COUNT):
            start_col = (sources[index_of_slot] * TILE_STRINGS).astype(jnp.int32)
            piece = lax.dynamic_slice_in_dim(coeffs, start_col, TILE_STRINGS, 1)
            total = total + product(piece, blocks[index_of_slot])
        return total

    column_list = lax.map(one_column, jnp.arange(TILE_COUNT, dtype=jnp.int32))
    halfsum = jnp.transpose(column_list, (1, 0, 2)).reshape(W, W)
    return halfsum + halfsum.T
```

```python
import functools

import jax
import jax.numpy as jnp
from jax import lax
from jax.experimental import pallas as pl
from jax.experimental.pallas import tpu as pltpu
from jax.sharding import PartitionSpec as P

MESH = pl.DeviceIdType.MESH
AHEAD = 2


def kernel(sizes, source_ref, present_ref, c_ref, m_ref, out_ref, *scratch):
    row_devices, col_devices, chunks = sizes
    gathered = scratch[:chunks]
    high, low, half, mirror, g_send, g_recv, x_send, x_recv = scratch[chunks:]
    tile = c_ref.shape[1]
    pair = c_ref.shape[0] // tile
    rows = c_ref.shape[0] // chunks
    per_tile = tile // rows
    slots = m_ref.shape[1]
    blocks = present_ref.shape[2]
    block = tile // blocks
    r, c = lax.axis_index("row"), lax.axis_index("col")
    planes = col_devices // 4
    across = c ^ 2
    sibling = c ^ 1
    ups = [lax.rem(c + 4 * step, col_devices) for step in range(1, planes)]
    partners = [(c // pair, r * pair + u) for u in range(pair)]
    own_tile = lax.rem(c, pair)
    on_diagonal = c // pair == r

    barrier = pltpu.get_barrier_semaphore()
    for peer in [across, sibling] + ups:
        pl.semaphore_signal(barrier, inc=1, device_id=(r, peer), device_id_type=MESH)
    for u, partner in enumerate(partners):
        @pl.when(jnp.logical_not(on_diagonal & (own_tile == u)))
        def _(partner=partner):
            pl.semaphore_signal(barrier, inc=1, device_id=partner, device_id_type=MESH)
    expected = planes + 1 + pair
    pl.semaphore_wait(barrier, jnp.where(on_diagonal, expected - 1, expected))

    def where(k):
        return (k % pair) * tile + (k // pair) * rows

    sent = []
    counts = [0] * chunks

    def send(k, src, origin, target):
        copy = pltpu.make_async_remote_copy(
            src_ref=src, dst_ref=gathered[k].at[origin],
            send_sem=g_send.at[k, counts[k]], recv_sem=g_recv.at[k, origin],
            device_id=(r, target), device_id_type=MESH)
        counts[k] += 1
        copy.start()
        sent.append(copy)

    def arrived(k, origin):
        pltpu.make_async_remote_copy(
            src_ref=gathered[k].at[origin], dst_ref=gathered[k].at[origin],
            send_sem=g_send.at[k, 0], recv_sem=g_recv.at[k, origin],
            device_id=(r, sibling), device_id_type=MESH).wait_recv()

    def stage_own(k):
        mine = c_ref.at[pl.ds(where(k), rows)]
        send(k, mine, c, across)
        for up in ups:
            send(k, mine, c, up)
        send(k, mine, c, sibling)

    def stage_pass(k):
        arrived(k, across)
        if k % 2 == 0:
            for up in ups:
                send(k, gathered[k].at[across], across, up)
        send(k, gathered[k].at[across], across, sibling)
        for up in ups:
            arrived(k, up)
            if k % 2 == 1:
                send(k, gathered[k].at[up], up, across)
            send(k, gathered[k].at[up], up, sibling)

    def stage_far(k):
        for up in ups:
            arrived(k, up ^ 2)
            send(k, gathered[k].at[up ^ 2], up ^ 2, sibling)

    def exchange(u, j):
        span = pl.ds(j * rows, rows)
        return pltpu.make_async_remote_copy(
            src_ref=half.at[u, span], dst_ref=mirror.at[own_tile, span],
            send_sem=x_send.at[u, j], recv_sem=x_recv.at[own_tile, j],
            device_id=partners[u], device_id_type=MESH)

    def stage_multiply(k):
        arrived(k, sibling)
        arrived(k, sibling ^ 2)
        for up in ups:
            arrived(k, up ^ 1)
            arrived(k, up ^ 3)
        total = None
        for m in range(slots):
            x = c_ref[pl.ds(where(k), rows), :] if m == 0 else gathered[k][source_ref[0, m - 1]]
            x_high = x.astype(jnp.bfloat16)
            x_low = (x - x_high.astype(jnp.float32)).astype(jnp.bfloat16)
            for a, b in ((x_high, high), (x_low, high), (x_high, low)):
                term = jnp.dot(a, b[m], preferred_element_type=jnp.float32)
                total = term if total is None else total + term
        u, j = k % pair, k // pair
        span = pl.ds(j * rows, rows)
        half[u, span, :] = total
        local = on_diagonal & (own_tile == u)

        @pl.when(local)
        def _():
            mirror[u, span, :] = total

        @pl.when(jnp.logical_not(local))
        def _():
            exchange(u, j).start()

    for k in range(min(AHEAD, chunks)):
        stage_own(k)

    @pl.loop(0, slots)
    def _(m):
        for i in range(blocks):
            for j in range(blocks):
                place = (m, pl.ds(i * block, block), pl.ds(j * block, block))
                kept = m_ref[(0,) + place] * present_ref[0, m, i, j].astype(jnp.float32)
                top = kept.astype(jnp.bfloat16)
                high[place] = top
                low[place] = (kept - top.astype(jnp.float32)).astype(jnp.bfloat16)

    for step in range(chunks + 2):
        if step + AHEAD < chunks:
            stage_own(step + AHEAD)
        if step < chunks:
            stage_pass(step)
        if 0 <= step - 1 < chunks:
            stage_far(step - 1)
        if step >= 2:
            stage_multiply(step - 2)

    for j in range(per_tile):
        for u in range(pair):
            local = on_diagonal & (own_tile == u)
            span = pl.ds(j * rows, rows)

            @pl.when(jnp.logical_not(local))
            def _():
                pltpu.make_async_remote_copy(
                    src_ref=half.at[u, span], dst_ref=mirror.at[u, span],
                    send_sem=x_send.at[u, j], recv_sem=x_recv.at[u, j],
                    device_id=partners[u], device_id_type=MESH).wait_recv()

            out_ref[pl.ds(u * tile, tile), span] = half[u, :, span] + mirror[u, span, :].T

    for copy in sent:
        copy.wait_send()
    for j in range(per_tile):
        for u in range(pair):
            @pl.when(jnp.logical_not(on_diagonal & (own_tile == u)))
            def _():
                exchange(u, j).wait_send()


def on_device(row_devices, col_devices, coeffs, hamiltonian_tiles, source_lists, present):
    height, tile = coeffs.shape
    slots = hamiltonian_tiles.shape[1]
    pair = height // tile
    rows = min(tile, 128)
    chunks = height // rows
    planes = col_devices // 4
    sends = 4 * planes - 1
    return pl.pallas_call(
        functools.partial(kernel, (row_devices, col_devices, chunks)),
        out_shape=jax.ShapeDtypeStruct(coeffs.shape, jnp.float32),
        in_specs=[pl.BlockSpec(memory_space=pltpu.SMEM)] * 2
        + [pl.BlockSpec(memory_space=pltpu.VMEM)] * 2,
        out_specs=pl.BlockSpec(memory_space=pltpu.VMEM),
        scratch_shapes=[pltpu.VMEM((col_devices, rows, tile), jnp.float32) for _ in range(chunks)]
        + [
            pltpu.VMEM((slots, tile, tile), jnp.bfloat16),
            pltpu.VMEM((slots, tile, tile), jnp.bfloat16),
            pltpu.VMEM((pair, tile, tile), jnp.float32),
            pltpu.VMEM((pair, tile, tile), jnp.float32),
            pltpu.SemaphoreType.DMA((chunks, sends)),
            pltpu.SemaphoreType.DMA((chunks, col_devices)),
            pltpu.SemaphoreType.DMA((pair, tile // rows)),
            pltpu.SemaphoreType.DMA((pair, tile // rows)),
        ],
        compiler_params=pltpu.CompilerParams(
            collective_id=0, has_side_effects=True, vmem_limit_bytes=60 * 2**20),
    )(source_lists, present, coeffs, hamiltonian_tiles)


def solution(mesh):
    placed = (
        P("row", "col"),
        P("col", None, None, None),
        P("col", None),
        P("col", None, None, None),
    )
    body = functools.partial(on_device, mesh.shape["row"], mesh.shape["col"])
    return jax.shard_map(
        body, mesh=mesh, in_specs=placed, out_specs=P("row", "col"), check_vma=False
    )
```

```python
import functools

import jax
import jax.numpy as jnp
from jax import lax
from jax.experimental import pallas as pl
from jax.experimental.pallas import tpu as pltpu
from jax.sharding import PartitionSpec as P

MESH = pl.DeviceIdType.MESH
AHEAD = 2
DELAY = 1


def kernel(sizes, source_ref, present_ref, c_ref, m_ref, out_ref, *scratch):
    row_devices, col_devices, chunks = sizes
    gathered = scratch[:chunks]
    (high, low, half, mirror, first, second, g_send, g_recv, x_send, x_recv,
     first_send, first_recv, second_send, second_recv) = scratch[chunks:]
    tile = c_ref.shape[1]
    pair = c_ref.shape[0] // tile
    rows = c_ref.shape[0] // chunks
    per_tile = tile // rows
    slots = m_ref.shape[1]
    blocks = present_ref.shape[2]
    block = tile // blocks
    r, c = lax.axis_index("row"), lax.axis_index("col")
    planes = col_devices // 4
    across = c ^ 2
    sibling = c ^ 1
    ups = [lax.rem(c + 4 * step, col_devices) for step in range(1, planes)]
    chip, core = c // pair, lax.rem(c, pair)
    apart = r ^ chip
    lowest = apart & (0 - apart)
    one_bit = (apart != 0) & (apart == lowest)
    on_diagonal = apart == 0

    barrier = pltpu.get_barrier_semaphore()
    for step in range(1, col_devices):
        peer = lax.rem(c + step, col_devices)
        pl.semaphore_signal(barrier, inc=1, device_id=(r, peer), device_id_type=MESH)
    for step in range(1, row_devices):
        for other in range(pair):
            peer = (lax.rem(r + step, row_devices), chip * pair + other)
            pl.semaphore_signal(barrier, inc=1, device_id=peer, device_id_type=MESH)
    pl.semaphore_wait(barrier, col_devices - 1 + pair * (row_devices - 1))

    def where(k):
        return (k % pair) * tile + (k // pair) * rows

    sent = []
    counts = [0] * chunks

    def send(k, src, origin, target):
        copy = pltpu.make_async_remote_copy(
            src_ref=src, dst_ref=gathered[k].at[origin],
            send_sem=g_send.at[k, counts[k]], recv_sem=g_recv.at[k, origin],
            device_id=(r, target), device_id_type=MESH)
        counts[k] += 1
        copy.start()
        sent.append(copy)

    def arrived(k, origin):
        pltpu.make_async_remote_copy(
            src_ref=gathered[k].at[origin], dst_ref=gathered[k].at[origin],
            send_sem=g_send.at[k, 0], recv_sem=g_recv.at[k, origin],
            device_id=(r, sibling), device_id_type=MESH).wait_recv()

    def stage_own(k):
        mine = c_ref.at[pl.ds(where(k), rows)]
        send(k, mine, c, across)
        for up in ups:
            send(k, mine, c, up)
        send(k, mine, c, sibling)

    def stage_pass(k):
        arrived(k, across)
        if k % 2 == 0:
            for up in ups:
                send(k, gathered[k].at[across], across, up)
        send(k, gathered[k].at[across], across, sibling)
        for up in ups:
            arrived(k, up)
            if k % 2 == 1:
                send(k, gathered[k].at[up], up, across)
            send(k, gathered[k].at[up], up, sibling)

    def stage_far(k):
        for up in ups:
            arrived(k, up ^ 2)
            send(k, gathered[k].at[up ^ 2], up ^ 2, sibling)

    def piece(j, route):
        return pl.ds(j * rows + route * (rows // 2), rows // 2)

    def source(u, j, route, act):
        def go(dst, landed, target):
            act(pltpu.make_async_remote_copy(
                src_ref=half.at[u, piece(j, route)], dst_ref=dst,
                send_sem=x_send.at[u, j, route], recv_sem=landed,
                device_id=target, device_id_type=MESH))

        @pl.when(on_diagonal & (core != u))
        def _():
            go(mirror.at[core, piece(j, route)], x_recv.at[core, j, route], (r, chip * pair + u))

        bent = jnp.logical_not(on_diagonal) if route == 0 else jnp.logical_not(on_diagonal | one_bit)
        via = chip ^ lowest if route == 0 else r ^ lowest

        @pl.when(bent)
        def _():
            go(first.at[apart // 2, core, j], first_recv.at[apart // 2, core, j], (r, via * pair + u))

        if route == 1:
            @pl.when(one_bit)
            def _():
                go(second.at[apart // 2, core, j], second_recv.at[apart // 2, core, j],
                   (chip, chip * pair + u))

    def relay_first(j, forward):
        for d in range(1, row_devices):
            low_bit = d & -d
            for route in range(2):
                at = d ^ low_bit if route == 0 else low_bit
                if at == d:
                    continue

                @pl.when(apart == at)
                def _(d=d, route=route, at=at):
                    for k in range(pair):
                        landing = first.at[d // 2, k, j]
                        if at == 0:
                            dst, landed = mirror.at[k, piece(j, route)], x_recv.at[k, j, route]
                        else:
                            dst, landed = second.at[d // 2, k, j], second_recv.at[d // 2, k, j]
                        forward(first_recv.at[d // 2, k, j], pltpu.make_async_remote_copy(
                            src_ref=landing, dst_ref=dst, send_sem=first_send.at[d // 2, k, j],
                            recv_sem=landed, device_id=(r ^ d, c), device_id_type=MESH), landing)

    def relay_second(j, forward):
        for d in range(1, row_devices):
            low_bit = d & -d
            for route in range(2):
                at = low_bit if route == 0 else d ^ low_bit
                if at == d:
                    continue

                @pl.when(apart == at)
                def _(d=d, route=route):
                    for k in range(pair):
                        landing = second.at[d // 2, k, j]
                        forward(second_recv.at[d // 2, k, j], pltpu.make_async_remote_copy(
                            src_ref=landing, dst_ref=mirror.at[k, piece(j, route)],
                            send_sem=second_send.at[d // 2, k, j], recv_sem=x_recv.at[k, j, route],
                            device_id=(r, (r ^ d) * pair + core), device_id_type=MESH), landing)

    def wait_landed(landed, ref):
        pltpu.make_async_remote_copy(
            src_ref=ref, dst_ref=ref, send_sem=x_send.at[0, 0, 0], recv_sem=landed,
            device_id=(r, sibling), device_id_type=MESH).wait_recv()

    def pass_on(landed, copy, landing):
        wait_landed(landed, landing)
        copy.start()

    def finish(landed, copy, landing):
        copy.wait_send()

    def stage_multiply(k):
        arrived(k, sibling)
        arrived(k, sibling ^ 2)
        for up in ups:
            arrived(k, up ^ 1)
            arrived(k, up ^ 3)
        total = None
        for m in range(slots):
            x = c_ref[pl.ds(where(k), rows), :] if m == 0 else gathered[k][source_ref[0, m - 1]]
            x_high = x.astype(jnp.bfloat16)
            x_low = (x - x_high.astype(jnp.float32)).astype(jnp.bfloat16)
            for a, b in ((x_high, high), (x_low, high), (x_high, low)):
                term = jnp.dot(a, b[m], preferred_element_type=jnp.float32)
                total = term if total is None else total + term
        u, j = k % pair, k // pair
        span = pl.ds(j * rows, rows)
        half[u, span, :] = total

        @pl.when(on_diagonal & (core == u))
        def _():
            mirror[u, span, :] = total

        for route in range(2):
            source(u, j, route, lambda copy: copy.start())

    for k in range(min(AHEAD, chunks)):
        stage_own(k)

    @pl.loop(0, slots)
    def _(m):
        for i in range(blocks):
            for j in range(blocks):
                place = (m, pl.ds(i * block, block), pl.ds(j * block, block))
                kept = m_ref[(0,) + place] * present_ref[0, m, i, j].astype(jnp.float32)
                top = kept.astype(jnp.bfloat16)
                high[place] = top
                low[place] = (kept - top.astype(jnp.float32)).astype(jnp.bfloat16)

    for step in range(chunks + 2 + DELAY * 2):
        if step + AHEAD < chunks:
            stage_own(step + AHEAD)
        if step < chunks:
            stage_pass(step)
        if 0 <= step - 1 < chunks:
            stage_far(step - 1)
        if 0 <= step - 2 < chunks:
            stage_multiply(step - 2)
        done = step - 2 - DELAY
        if done >= 0 and done % pair == pair - 1 and done // pair < per_tile:
            relay_first(done // pair, pass_on)
        done -= DELAY
        if done >= 0 and done % pair == pair - 1 and done // pair < per_tile:
            relay_second(done // pair, pass_on)

    for j in range(per_tile):
        for u in range(pair):
            span = pl.ds(j * rows, rows)

            @pl.when(jnp.logical_not(on_diagonal & (core == u)))
            def _():
                for route in range(2):
                    wait_landed(x_recv.at[u, j, route], mirror.at[u, piece(j, route)])

            out_ref[pl.ds(u * tile, tile), span] = half[u, :, span] + mirror[u, span, :].T

    for copy in sent:
        copy.wait_send()
    for j in range(per_tile):
        for u in range(pair):
            for route in range(2):
                source(u, j, route, lambda copy: copy.wait_send())
        relay_first(j, finish)
        relay_second(j, finish)


def on_device(row_devices, col_devices, coeffs, hamiltonian_tiles, source_lists, present):
    height, tile = coeffs.shape
    slots = hamiltonian_tiles.shape[1]
    pair = height // tile
    rows = min(tile, 128)
    chunks = height // rows
    planes = col_devices // 4
    sends = 4 * planes - 1
    relayed = (row_devices // 2, pair, tile // rows)
    return pl.pallas_call(
        functools.partial(kernel, (row_devices, col_devices, chunks)),
        out_shape=jax.ShapeDtypeStruct(coeffs.shape, jnp.float32),
        in_specs=[pl.BlockSpec(memory_space=pltpu.SMEM)] * 2
        + [pl.BlockSpec(memory_space=pltpu.VMEM)] * 2,
        out_specs=pl.BlockSpec(memory_space=pltpu.VMEM),
        scratch_shapes=[pltpu.VMEM((col_devices, rows, tile), jnp.float32) for _ in range(chunks)]
        + [
            pltpu.VMEM((slots, tile, tile), jnp.bfloat16),
            pltpu.VMEM((slots, tile, tile), jnp.bfloat16),
            pltpu.VMEM((pair, tile, tile), jnp.float32),
            pltpu.VMEM((pair, tile, tile), jnp.float32),
            pltpu.VMEM(relayed + (rows // 2, tile), jnp.float32),
            pltpu.VMEM(relayed + (rows // 2, tile), jnp.float32),
            pltpu.SemaphoreType.DMA((chunks, sends)),
            pltpu.SemaphoreType.DMA((chunks, col_devices)),
            pltpu.SemaphoreType.DMA((pair, tile // rows, 2)),
            pltpu.SemaphoreType.DMA((pair, tile // rows, 2)),
            pltpu.SemaphoreType.DMA(relayed),
            pltpu.SemaphoreType.DMA(relayed),
            pltpu.SemaphoreType.DMA(relayed),
            pltpu.SemaphoreType.DMA(relayed),
        ],
        compiler_params=pltpu.CompilerParams(
            collective_id=0, has_side_effects=True, vmem_limit_bytes=60 * 2**20),
    )(source_lists, present, coeffs, hamiltonian_tiles)


def solution(mesh):
    placed = (
        P("row", "col"),
        P("col", None, None, None),
        P("col", None),
        P("col", None, None, None),
    )
    body = functools.partial(on_device, mesh.shape["row"], mesh.shape["col"])
    return jax.shard_map(
        body, mesh=mesh, in_specs=placed, out_specs=P("row", "col"), check_vma=False
    )
```

```python
import functools

import jax
import jax.numpy as jnp
from jax import lax
from jax.experimental import pallas as pl
from jax.experimental.pallas import tpu as pltpu
from jax.sharding import PartitionSpec as P

MESH = pl.DeviceIdType.MESH
AHEAD = 2
DELAY = 1
LAST = 2


def kernel(sizes, source_ref, present_ref, c_hbm, m_hbm, out_hbm, *scratch):
    row_devices, col_devices, segments = sizes
    tile = c_hbm.shape[1]
    pair = c_hbm.shape[0] // tile
    chunks = pair * len(segments)
    per_tile = len(segments)
    gathered = scratch[:chunks]
    (high, low, half, mirror, first, second, g_send, g_recv, x_send, x_recv,
     first_send, first_recv, second_send, second_recv,
     c_ref, m_ref, out_ref, c_done, m_done, out_done) = scratch[chunks:]
    slots = m_hbm.shape[1]
    blocks = present_ref.shape[2]
    block = tile // blocks
    r, c = lax.axis_index("row"), lax.axis_index("col")
    planes = col_devices // 4
    across = c ^ 2
    sibling = c ^ 1
    ups = [lax.rem(c + 4 * step, col_devices) for step in range(1, planes)]
    chip, core = c // pair, lax.rem(c, pair)
    apart = r ^ chip
    lowest = apart & (0 - apart)
    one_bit = (apart != 0) & (apart == lowest)
    on_diagonal = apart == 0

    c_copy = pltpu.make_async_copy(c_hbm, c_ref, c_done)
    c_copy.start()

    def m_copy(m):
        return pltpu.make_async_copy(m_hbm.at[0, m], m_ref.at[m], m_done.at[m])

    for m in range(slots):
        m_copy(m).start()

    barrier = pltpu.get_barrier_semaphore()
    for step in range(1, col_devices):
        peer = lax.rem(c + step, col_devices)
        pl.semaphore_signal(barrier, inc=1, device_id=(r, peer), device_id_type=MESH)
    for step in range(1, row_devices):
        for other in range(pair):
            peer = (lax.rem(r + step, row_devices), chip * pair + other)
            pl.semaphore_signal(barrier, inc=1, device_id=peer, device_id_type=MESH)
    pl.semaphore_wait(barrier, col_devices - 1 + pair * (row_devices - 1))

    def where(k):
        first_row, rows = segments[k // pair]
        return pl.ds((k % pair) * tile + first_row, rows)

    sent = []
    counts = [0] * chunks

    def send(k, src, origin, target):
        copy = pltpu.make_async_remote_copy(
            src_ref=src, dst_ref=gathered[k].at[origin],
            send_sem=g_send.at[k, counts[k]], recv_sem=g_recv.at[k, origin],
            device_id=(r, target), device_id_type=MESH)
        counts[k] += 1
        copy.start()
        sent.append(copy)

    def arrived(k, origin):
        pltpu.make_async_remote_copy(
            src_ref=gathered[k].at[origin], dst_ref=gathered[k].at[origin],
            send_sem=g_send.at[k, 0], recv_sem=g_recv.at[k, origin],
            device_id=(r, sibling), device_id_type=MESH).wait_recv()

    def stage_own(k):
        mine = c_hbm.at[where(k)]
        send(k, mine, c, across)
        for up in ups:
            send(k, mine, c, up)
        send(k, mine, c, sibling)

    def stage_pass(k):
        arrived(k, across)
        if k % 2 == 0:
            for up in ups:
                send(k, gathered[k].at[across], across, up)
        send(k, gathered[k].at[across], across, sibling)
        for up in ups:
            arrived(k, up)
            if k % 2 == 1:
                send(k, gathered[k].at[up], up, across)
            send(k, gathered[k].at[up], up, sibling)

    def stage_far(k):
        for up in ups:
            arrived(k, up ^ 2)
            send(k, gathered[k].at[up ^ 2], up ^ 2, sibling)

    def piece(j, route):
        first_row, rows = segments[j]
        return pl.ds(first_row + route * (rows // 2), rows // 2)

    def relayed(j):
        first_row, rows = segments[j]
        return pl.ds(first_row // 2, rows // 2)

    def source(u, j, route, act):
        def go(dst, landed, target):
            act(pltpu.make_async_remote_copy(
                src_ref=half.at[u, piece(j, route)], dst_ref=dst,
                send_sem=x_send.at[u, j, route], recv_sem=landed,
                device_id=target, device_id_type=MESH))

        @pl.when(on_diagonal & (core != u))
        def _():
            go(mirror.at[core, piece(j, route)], x_recv.at[core, j, route], (r, chip * pair + u))

        bent = jnp.logical_not(on_diagonal) if route == 0 else jnp.logical_not(on_diagonal | one_bit)
        via = chip ^ lowest if route == 0 else r ^ lowest

        @pl.when(bent)
        def _():
            go(first.at[apart // 2, core, relayed(j)], first_recv.at[apart // 2, core, j], (r, via * pair + u))

        if route == 1:
            @pl.when(one_bit)
            def _():
                go(second.at[apart // 2, core, relayed(j)], second_recv.at[apart // 2, core, j],
                   (chip, chip * pair + u))

    def relay_first(j, forward):
        for d in range(1, row_devices):
            low_bit = d & -d
            for route in range(2):
                at = d ^ low_bit if route == 0 else low_bit
                if at == d:
                    continue

                @pl.when(apart == at)
                def _(d=d, route=route, at=at):
                    for k in range(pair):
                        landing = first.at[d // 2, k, relayed(j)]
                        if at == 0:
                            dst, landed = mirror.at[k, piece(j, route)], x_recv.at[k, j, route]
                        else:
                            dst, landed = second.at[d // 2, k, relayed(j)], second_recv.at[d // 2, k, j]
                        forward(first_recv.at[d // 2, k, j], pltpu.make_async_remote_copy(
                            src_ref=landing, dst_ref=dst, send_sem=first_send.at[d // 2, k, j],
                            recv_sem=landed, device_id=(r ^ d, c), device_id_type=MESH), landing)

    def relay_second(j, forward):
        for d in range(1, row_devices):
            low_bit = d & -d
            for route in range(2):
                at = low_bit if route == 0 else d ^ low_bit
                if at == d:
                    continue

                @pl.when(apart == at)
                def _(d=d, route=route):
                    for k in range(pair):
                        landing = second.at[d // 2, k, relayed(j)]
                        forward(second_recv.at[d // 2, k, j], pltpu.make_async_remote_copy(
                            src_ref=landing, dst_ref=mirror.at[k, piece(j, route)],
                            send_sem=second_send.at[d // 2, k, j], recv_sem=x_recv.at[k, j, route],
                            device_id=(r, (r ^ d) * pair + core), device_id_type=MESH), landing)

    def wait_landed(landed, ref):
        pltpu.make_async_remote_copy(
            src_ref=ref, dst_ref=ref, send_sem=x_send.at[0, 0, 0], recv_sem=landed,
            device_id=(r, sibling), device_id_type=MESH).wait_recv()

    def pass_on(landed, copy, landing):
        wait_landed(landed, landing)
        copy.start()

    def finish(landed, copy, landing):
        copy.wait_send()

    def stage_multiply(k):
        arrived(k, sibling)
        arrived(k, sibling ^ 2)
        for up in ups:
            arrived(k, up ^ 1)
            arrived(k, up ^ 3)
        rows = segments[k // pair][1]
        total = None
        for m in range(slots):
            x = c_ref[where(k), :] if m == 0 else gathered[k][source_ref[0, m - 1]]
            x_high = x.astype(jnp.bfloat16)
            x_low = (x - x_high.astype(jnp.float32)).astype(jnp.bfloat16)
            both = jnp.dot(jnp.concatenate([x_high, x_low], axis=0), high[m],
                           preferred_element_type=jnp.float32)
            term = both[:rows] + both[rows:] + jnp.dot(
                x_high, low[m], preferred_element_type=jnp.float32)
            total = term if total is None else total + term
        u, j = k % pair, k // pair
        span = pl.ds(*segments[j])
        half[u, span, :] = total

        @pl.when(on_diagonal & (core == u))
        def _():
            mirror[u, span, :] = total

        for route in range(2):
            source(u, j, route, lambda copy: copy.start())

    for k in range(min(AHEAD, chunks)):
        stage_own(k)

    @pl.loop(0, slots)
    def _(m):
        m_copy(m).wait()
        for i in range(blocks):
            for j in range(blocks):
                place = (m, pl.ds(i * block, block), pl.ds(j * block, block))
                kept = m_ref[place] * present_ref[0, m, i, j].astype(jnp.float32)
                top = kept.astype(jnp.bfloat16)
                high[place] = top
                low[place] = (kept - top.astype(jnp.float32)).astype(jnp.bfloat16)

    c_copy.wait()
    for step in range(chunks + 2 + DELAY * 2):
        if step + AHEAD < chunks:
            stage_own(step + AHEAD)
        if step < chunks:
            stage_pass(step)
        if 0 <= step - 1 < chunks:
            stage_far(step - 1)
        if 0 <= step - 2 < chunks:
            stage_multiply(step - 2)
        done = step - 2 - DELAY
        if done >= 0 and done % pair == pair - 1 and done // pair < per_tile:
            relay_first(done // pair, pass_on)
        done -= DELAY
        if done >= 0 and done % pair == pair - 1 and done // pair < per_tile:
            relay_second(done // pair, pass_on)

    written = []
    for first_row in range(0, tile, block):
        for u in range(pair):
            span = pl.ds(first_row, block)

            @pl.when(jnp.logical_not(on_diagonal & (core == u)))
            def _():
                for j in range(per_tile):
                    if first_row <= segments[j][0] < first_row + block:
                        for route in range(2):
                            wait_landed(x_recv.at[u, j, route], mirror.at[u, piece(j, route)])

            place = (pl.ds(u * tile, tile), span)
            out_ref[place] = half[u, :, span] + mirror[u, span, :].T
            copy = pltpu.make_async_copy(
                out_ref.at[place], out_hbm.at[place], out_done.at[u, first_row // block])
            copy.start()
            written.append(copy)

    for copy in written:
        copy.wait()
    for copy in sent:
        copy.wait_send()
    for j in range(per_tile):
        for u in range(pair):
            for route in range(2):
                source(u, j, route, lambda copy: copy.wait_send())
        relay_first(j, finish)
        relay_second(j, finish)


def on_device(row_devices, col_devices, coeffs, hamiltonian_tiles, source_lists, present):
    height, tile = coeffs.shape
    slots = hamiltonian_tiles.shape[1]
    pair = height // tile
    block = tile // present.shape[-1]
    segments = []
    for first_row in range(0, tile, block):
        parts = 1 if first_row + block < tile else LAST
        segments += [(first_row + i * (block // parts), block // parts) for i in range(parts)]
    chunks = pair * len(segments)
    planes = col_devices // 4
    sends = 4 * planes - 1
    relayed = (row_devices // 2, pair, len(segments))
    return pl.pallas_call(
        functools.partial(kernel, (row_devices, col_devices, tuple(segments))),
        out_shape=jax.ShapeDtypeStruct(coeffs.shape, jnp.float32),
        in_specs=[pl.BlockSpec(memory_space=pltpu.SMEM)] * 2
        + [pl.BlockSpec(memory_space=pl.ANY)] * 2,
        out_specs=pl.BlockSpec(memory_space=pl.ANY),
        scratch_shapes=[
            pltpu.VMEM((col_devices, segments[k // pair][1], tile), jnp.float32)
            for k in range(chunks)
        ]
        + [
            pltpu.VMEM((slots, tile, tile), jnp.bfloat16),
            pltpu.VMEM((slots, tile, tile), jnp.bfloat16),
            pltpu.VMEM((pair, tile, tile), jnp.float32),
            pltpu.VMEM((pair, tile, tile), jnp.float32),
            pltpu.VMEM(relayed[:2] + (tile // 2, tile), jnp.float32),
            pltpu.VMEM(relayed[:2] + (tile // 2, tile), jnp.float32),
            pltpu.SemaphoreType.DMA((chunks, sends)),
            pltpu.SemaphoreType.DMA((chunks, col_devices)),
            pltpu.SemaphoreType.DMA((pair, len(segments), 2)),
            pltpu.SemaphoreType.DMA((pair, len(segments), 2)),
            pltpu.SemaphoreType.DMA(relayed),
            pltpu.SemaphoreType.DMA(relayed),
            pltpu.SemaphoreType.DMA(relayed),
            pltpu.SemaphoreType.DMA(relayed),
            pltpu.VMEM(coeffs.shape, jnp.float32),
            pltpu.VMEM((slots, tile, tile), jnp.float32),
            pltpu.VMEM(coeffs.shape, jnp.float32),
            pltpu.SemaphoreType.DMA,
            pltpu.SemaphoreType.DMA((slots,)),
            pltpu.SemaphoreType.DMA((pair, tile // block)),
        ],
        compiler_params=pltpu.CompilerParams(
            collective_id=0, has_side_effects=True, vmem_limit_bytes=60 * 2**20),
    )(source_lists, present, coeffs, hamiltonian_tiles)


def solution(mesh):
    placed = (
        P("row", "col"),
        P("col", None, None, None),
        P("col", None),
        P("col", None, None, None),
    )
    body = functools.partial(on_device, mesh.shape["row"], mesh.shape["col"])
    return jax.shard_map(
        body, mesh=mesh, in_specs=placed, out_specs=P("row", "col"), check_vma=False
    )
```

```python
import functools

import jax
import jax.numpy as jnp
from jax import lax
from jax.experimental import pallas as pl
from jax.experimental.pallas import tpu as pltpu
from jax.sharding import PartitionSpec as P

MESH = pl.DeviceIdType.MESH
AHEAD = 2
DELAY = 1
PARTS = 2


def kernel(sizes, source_ref, present_ref, c_hbm, m_hbm, out_hbm, *scratch):
    row_devices, col_devices, segments = sizes
    tile = c_hbm.shape[1]
    pair = c_hbm.shape[0] // tile
    chunks = pair * len(segments)
    per_tile = len(segments)
    gathered = scratch[:chunks]
    (high, low, half, mirror, first, second, g_send, g_recv, x_send, x_recv,
     first_send, first_recv, second_send, second_recv,
     c_ref, m_ref, out_ref, c_done, m_done, out_done) = scratch[chunks:]
    slots = m_hbm.shape[1]
    blocks = present_ref.shape[2]
    block = tile // blocks
    r, c = lax.axis_index("row"), lax.axis_index("col")
    planes = col_devices // 4
    across = c ^ 2
    sibling = c ^ 1
    ups = [lax.rem(c + 4 * step, col_devices) for step in range(1, planes)]
    chip, core = c // pair, lax.rem(c, pair)
    apart = r ^ chip
    lowest = apart & (0 - apart)
    one_bit = (apart != 0) & (apart == lowest)
    on_diagonal = apart == 0

    c_copy = pltpu.make_async_copy(c_hbm, c_ref, c_done)
    c_copy.start()

    def m_copy(m):
        return pltpu.make_async_copy(m_hbm.at[0, m], m_ref.at[m], m_done.at[m])

    for m in range(slots):
        m_copy(m).start()

    barrier = pltpu.get_barrier_semaphore()
    for step in range(1, col_devices):
        peer = lax.rem(c + step, col_devices)
        pl.semaphore_signal(barrier, inc=1, device_id=(r, peer), device_id_type=MESH)
    for step in range(1, row_devices):
        for other in range(pair):
            peer = (lax.rem(r + step, row_devices), chip * pair + other)
            pl.semaphore_signal(barrier, inc=1, device_id=peer, device_id_type=MESH)
    pl.semaphore_wait(barrier, col_devices - 1 + pair * (row_devices - 1))

    def where(k):
        first_row, rows = segments[k // pair]
        return pl.ds((k % pair) * tile + first_row, rows)

    sent = []
    counts = [0] * chunks

    def send(k, src, origin, target):
        copy = pltpu.make_async_remote_copy(
            src_ref=src, dst_ref=gathered[k].at[origin],
            send_sem=g_send.at[k, counts[k]], recv_sem=g_recv.at[k, origin],
            device_id=(r, target), device_id_type=MESH)
        counts[k] += 1
        copy.start()
        sent.append(copy)

    def arrived(k, origin):
        pltpu.make_async_remote_copy(
            src_ref=gathered[k].at[origin], dst_ref=gathered[k].at[origin],
            send_sem=g_send.at[k, 0], recv_sem=g_recv.at[k, origin],
            device_id=(r, sibling), device_id_type=MESH).wait_recv()

    def stage_own(k):
        mine = c_hbm.at[where(k)]
        send(k, mine, c, across)
        for up in ups:
            send(k, mine, c, up)
        send(k, mine, c, sibling)

    def stage_pass(k):
        arrived(k, across)
        if k % 2 == 0:
            for up in ups:
                send(k, gathered[k].at[across], across, up)
        send(k, gathered[k].at[across], across, sibling)
        for up in ups:
            arrived(k, up)
            if k % 2 == 1:
                send(k, gathered[k].at[up], up, across)
            send(k, gathered[k].at[up], up, sibling)

    def stage_far(k):
        for up in ups:
            arrived(k, up ^ 2)
            send(k, gathered[k].at[up ^ 2], up ^ 2, sibling)

    def piece(j, route):
        first_row, rows = segments[j]
        return pl.ds(first_row + route * (rows // 2), rows // 2)

    def relayed(j):
        first_row, rows = segments[j]
        return pl.ds(first_row // 2, rows // 2)

    def source(u, j, route, act):
        def go(dst, landed, target):
            act(pltpu.make_async_remote_copy(
                src_ref=half.at[u, piece(j, route)], dst_ref=dst,
                send_sem=x_send.at[u, j, route], recv_sem=landed,
                device_id=target, device_id_type=MESH))

        @pl.when(on_diagonal & (core != u))
        def _():
            go(mirror.at[core, piece(j, route)], x_recv.at[core, j, route], (r, chip * pair + u))

        bent = jnp.logical_not(on_diagonal) if route == 0 else jnp.logical_not(on_diagonal | one_bit)
        via = chip ^ lowest if route == 0 else r ^ lowest

        @pl.when(bent)
        def _():
            go(first.at[apart // 2, core, relayed(j)], first_recv.at[apart // 2, core, j], (r, via * pair + u))

        if route == 1:
            @pl.when(one_bit)
            def _():
                go(second.at[apart // 2, core, relayed(j)], second_recv.at[apart // 2, core, j],
                   (chip, chip * pair + u))

    def relay_first(j, forward):
        for d in range(1, row_devices):
            low_bit = d & -d
            for route in range(2):
                at = d ^ low_bit if route == 0 else low_bit
                if at == d:
                    continue

                @pl.when(apart == at)
                def _(d=d, route=route, at=at):
                    for k in range(pair):
                        landing = first.at[d // 2, k, relayed(j)]
                        if at == 0:
                            dst, landed = mirror.at[k, piece(j, route)], x_recv.at[k, j, route]
                        else:
                            dst, landed = second.at[d // 2, k, relayed(j)], second_recv.at[d // 2, k, j]
                        forward(first_recv.at[d // 2, k, j], pltpu.make_async_remote_copy(
                            src_ref=landing, dst_ref=dst, send_sem=first_send.at[d // 2, k, j],
                            recv_sem=landed, device_id=(r ^ d, c), device_id_type=MESH), landing)

    def relay_second(j, forward):
        for d in range(1, row_devices):
            low_bit = d & -d
            for route in range(2):
                at = low_bit if route == 0 else d ^ low_bit
                if at == d:
                    continue

                @pl.when(apart == at)
                def _(d=d, route=route):
                    for k in range(pair):
                        landing = second.at[d // 2, k, relayed(j)]
                        forward(second_recv.at[d // 2, k, j], pltpu.make_async_remote_copy(
                            src_ref=landing, dst_ref=mirror.at[k, piece(j, route)],
                            send_sem=second_send.at[d // 2, k, j], recv_sem=x_recv.at[k, j, route],
                            device_id=(r, (r ^ d) * pair + core), device_id_type=MESH), landing)

    def wait_landed(landed, ref):
        pltpu.make_async_remote_copy(
            src_ref=ref, dst_ref=ref, send_sem=x_send.at[0, 0, 0], recv_sem=landed,
            device_id=(r, sibling), device_id_type=MESH).wait_recv()

    def pass_on(landed, copy, landing):
        wait_landed(landed, landing)
        copy.start()

    def finish(landed, copy, landing):
        copy.wait_send()

    def stage_multiply(k):
        arrived(k, sibling)
        arrived(k, sibling ^ 2)
        for up in ups:
            arrived(k, up ^ 1)
            arrived(k, up ^ 3)
        rows = segments[k // pair][1]
        total = None
        for m in range(slots):
            x = c_ref[where(k), :] if m == 0 else gathered[k][source_ref[0, m - 1]]
            x_high = x.astype(jnp.bfloat16)
            x_low = (x - x_high.astype(jnp.float32)).astype(jnp.bfloat16)
            both = jnp.dot(jnp.concatenate([x_high, x_low], axis=0), high[m],
                           preferred_element_type=jnp.float32)
            term = both[:rows] + both[rows:] + jnp.dot(
                x_high, low[m], preferred_element_type=jnp.float32)
            total = term if total is None else total + term
        u, j = k % pair, k // pair
        span = pl.ds(*segments[j])
        half[u, span, :] = total

        @pl.when(on_diagonal & (core == u))
        def _():
            mirror[u, span, :] = total

        for route in range(2):
            source(u, j, route, lambda copy: copy.start())

    for k in range(min(AHEAD, chunks)):
        stage_own(k)

    @pl.loop(0, slots)
    def _(m):
        m_copy(m).wait()
        for i in range(blocks):
            for j in range(blocks):
                place = (m, pl.ds(i * block, block), pl.ds(j * block, block))
                kept = m_ref[place] * present_ref[0, m, i, j].astype(jnp.float32)
                top = kept.astype(jnp.bfloat16)
                high[place] = top
                low[place] = (kept - top.astype(jnp.float32)).astype(jnp.bfloat16)

    c_copy.wait()
    for step in range(chunks + 2 + DELAY * 2):
        if step + AHEAD < chunks:
            stage_own(step + AHEAD)
        if step < chunks:
            stage_pass(step)
        if 0 <= step - 1 < chunks:
            stage_far(step - 1)
        if 0 <= step - 2 < chunks:
            stage_multiply(step - 2)
        done = step - 2 - DELAY
        if done >= 0 and done % pair == pair - 1 and done // pair < per_tile:
            relay_first(done // pair, pass_on)
        done -= DELAY
        if done >= 0 and done % pair == pair - 1 and done // pair < per_tile:
            relay_second(done // pair, pass_on)

    written = []
    for first_row in range(0, tile, block):
        for u in range(pair):
            span = pl.ds(first_row, block)

            @pl.when(jnp.logical_not(on_diagonal & (core == u)))
            def _():
                for j in range(per_tile):
                    if first_row <= segments[j][0] < first_row + block:
                        for route in range(2):
                            wait_landed(x_recv.at[u, j, route], mirror.at[u, piece(j, route)])

            place = (pl.ds(u * tile, tile), span)
            out_ref[place] = half[u, :, span] + mirror[u, span, :].T
            copy = pltpu.make_async_copy(
                out_ref.at[place], out_hbm.at[place], out_done.at[u, first_row // block])
            copy.start()
            written.append(copy)

    for copy in written:
        copy.wait()
    for copy in sent:
        copy.wait_send()
    for j in range(per_tile):
        for u in range(pair):
            for route in range(2):
                source(u, j, route, lambda copy: copy.wait_send())
        relay_first(j, finish)
        relay_second(j, finish)


def on_device(row_devices, col_devices, coeffs, hamiltonian_tiles, source_lists, present):
    height, tile = coeffs.shape
    slots = hamiltonian_tiles.shape[1]
    pair = height // tile
    block = tile // present.shape[-1]
    segments = []
    for first_row in range(0, tile, block):
        parts = PARTS
        segments += [(first_row + i * (block // parts), block // parts) for i in range(parts)]
    chunks = pair * len(segments)
    planes = col_devices // 4
    sends = 4 * planes - 1
    relayed = (row_devices // 2, pair, len(segments))
    return pl.pallas_call(
        functools.partial(kernel, (row_devices, col_devices, tuple(segments))),
        out_shape=jax.ShapeDtypeStruct(coeffs.shape, jnp.float32),
        in_specs=[pl.BlockSpec(memory_space=pltpu.SMEM)] * 2
        + [pl.BlockSpec(memory_space=pl.ANY)] * 2,
        out_specs=pl.BlockSpec(memory_space=pl.ANY),
        scratch_shapes=[
            pltpu.VMEM((col_devices, segments[k // pair][1], tile), jnp.float32)
            for k in range(chunks)
        ]
        + [
            pltpu.VMEM((slots, tile, tile), jnp.bfloat16),
            pltpu.VMEM((slots, tile, tile), jnp.bfloat16),
            pltpu.VMEM((pair, tile, tile), jnp.float32),
            pltpu.VMEM((pair, tile, tile), jnp.float32),
            pltpu.VMEM(relayed[:2] + (tile // 2, tile), jnp.float32),
            pltpu.VMEM(relayed[:2] + (tile // 2, tile), jnp.float32),
            pltpu.SemaphoreType.DMA((chunks, sends)),
            pltpu.SemaphoreType.DMA((chunks, col_devices)),
            pltpu.SemaphoreType.DMA((pair, len(segments), 2)),
            pltpu.SemaphoreType.DMA((pair, len(segments), 2)),
            pltpu.SemaphoreType.DMA(relayed),
            pltpu.SemaphoreType.DMA(relayed),
            pltpu.SemaphoreType.DMA(relayed),
            pltpu.SemaphoreType.DMA(relayed),
            pltpu.VMEM(coeffs.shape, jnp.float32),
            pltpu.VMEM((slots, tile, tile), jnp.float32),
            pltpu.VMEM(coeffs.shape, jnp.float32),
            pltpu.SemaphoreType.DMA,
            pltpu.SemaphoreType.DMA((slots,)),
            pltpu.SemaphoreType.DMA((pair, tile // block)),
        ],
        compiler_params=pltpu.CompilerParams(
            collective_id=0, has_side_effects=True, vmem_limit_bytes=60 * 2**20),
    )(source_lists, present, coeffs, hamiltonian_tiles)


def solution(mesh):
    placed = (
        P("row", "col"),
        P("col", None, None, None),
        P("col", None),
        P("col", None, None, None),
    )
    body = functools.partial(on_device, mesh.shape["row"], mesh.shape["col"])
    return jax.shard_map(
        body, mesh=mesh, in_specs=placed, out_specs=P("row", "col"), check_vma=False
    )
```
